32 devices in a mesh: row: 8 (over y, x, core), col: 4 (over z).
Axes of the slice: x: 2, y: 2, z: 4, core: 2. Of those that a mesh axis runs over, the one named last changes fastest.
Arguments:
- specimen_transmit: float32 [2, 2, 2048, 1024], P(None, None, 'row', 'col'), may hold values from -5 to 5
- illumination: float32 [2, 256, 256], replicated, may hold values from -5 to 5
- fresnel_angle: float32 [256, 256], replicated, may hold values from -3.140625 to 3.140625
- recorded_intensity: float32 [8, 4, 2, 256, 256], P('row', 'col'), may hold values from 0.1 to 3
- frame_shifts: int32 [8, 4, 2, 2], P('row', 'col'), may hold values from -128 to 128, as said below
Outputs:
- obj_grad: float32 [2, 2, 2048, 1024], P(None, None, 'row', 'col')
- probe_grad: float32 [2, 256, 256], P(None, 'row', 'col')
The draws below stay inside these ranges and needn't reach their ends.
Inputs may be any that keep to these rules, and one draw needn't show every extreme that they name: `frame_shifts`: shifts stay within the margin, so a window reaches only its own tile and the eight tiles around it; both ends of the range occur in every draw.
All inputs are finite; a program needn't handle non-finite values.
Results may differ from the reference program's by a relative error of at most 0.0003.
Values sent between devices are 32-bit elements; how exact they have to be, the bound alone decides.
A program may use at most 128 MiB of HBM per device.

```python
import math
import jax
import jax.numpy as jnp
from jax import lax

FRAME_WIDTH = 256
HALO = 128
SLICES = 2
SCAN_STOPS = 2
TILE = 256
BRICKS_DOWN = 8
BRICKS_ACROSS = 4
NR = 2048
NC = 1024


def draw_frame_shifts(key, part):
    lowest = 0 - HALO
    highest = TILE + HALO - FRAME_WIDTH
    values = jax.random.randint(jax.random.fold_in(key, 11), (BRICKS_DOWN, BRICKS_ACROSS, SCAN_STOPS, 2), lowest, highest + 1)
    pick_rows = jax.random.randint(jax.random.fold_in(key, 12), (2,), 0, BRICKS_DOWN)
    pick_cols = jax.random.randint(jax.random.fold_in(key, 13), (2,), 0, BRICKS_ACROSS)
    values = values.at[pick_rows[0], pick_cols[0], 0, 0].set(lowest)
    values = values.at[pick_rows[1], pick_cols[1], SCAN_STOPS - 1, 1].set(highest)
    return values.astype(jnp.int32)


def block_scale(stream_key, shape, split, low, largest):
    level, own = 1.0, jax.random.fold_in(stream_key, 6)
    for position, blocks in split:
        draws = jnp.exp(jax.random.uniform(jax.random.fold_in(own, position), (blocks,), jnp.float32, low / len(split), largest / len(split)))
        level = level * jnp.repeat(draws, shape[position] // blocks).reshape([-1 if axis == position else 1 for axis in range(len(shape))])
    return level


def centred(stream_key, extent, scale, bound, split=(), held_as=jnp.bfloat16):
    gain = block_scale(stream_key, extent, split, -0.22, 0.18) if split else 1.0
    values = jax.random.normal(stream_key, extent, jnp.float32) * scale * gain
    return jnp.minimum(jnp.maximum(values, -bound), bound).astype(held_as)


def setup_inputs(seed: int = 0) -> dict:
    key_of = jax.random.split(jax.random.key(seed), 6)
    specimen_transmit = centred(key_of[0], (SLICES, 2, NR, NC), 0.7, 5.0, ((2, 8), (3, 4)), jnp.float32)
    illumination = centred(key_of[1], (2, FRAME_WIDTH, FRAME_WIDTH), 0.7, 5.0, (), jnp.float32)
    fresnel_angle = jnp.clip(jax.random.uniform(key_of[2], (FRAME_WIDTH, FRAME_WIDTH), jnp.float32, -3.140625, 3.140625), -3.140625, 3.140625)
    recorded_intensity = jnp.clip(jnp.exp(math.log(3.0) - 3.4011974 * jax.random.uniform(key_of[3], (BRICKS_DOWN, BRICKS_ACROSS, SCAN_STOPS, FRAME_WIDTH, FRAME_WIDTH), jnp.float32) ** block_scale(key_of[3], (BRICKS_DOWN, BRICKS_ACROSS, SCAN_STOPS, FRAME_WIDTH, FRAME_WIDTH), ((0, 8), (1, 4)), -0.2, 0.2)), 0.1, 3.0)
    frame_shifts = draw_frame_shifts(jax.random.fold_in(key_of[5], 71), 0)
    return dict(specimen_transmit=specimen_transmit, illumination=illumination, fresnel_angle=fresnel_angle, recorded_intensity=recorded_intensity, frame_shifts=frame_shifts)


def complex_product(a_real, a_imag, b_real, b_imag):
    return a_real * b_real - a_imag * b_imag, a_real * b_imag + a_imag * b_real


def conj_product(a_real, a_imag, b_real, b_imag):
    return a_real * b_real + a_imag * b_imag, a_real * b_imag - a_imag * b_real


def forward_dft(real_part, imag_part):
    result = jnp.fft.fft2(real_part + 1j * imag_part, norm="ortho")
    return jnp.real(result), jnp.imag(result)


def inverse_dft(real_part, imag_part):
    result = jnp.fft.ifft2(real_part + 1j * imag_part, norm="ortho")
    return jnp.real(result), jnp.imag(result)


def location_derivative(illuminated_frame, illumination, filter_inphase, filter_quadrature, observed_intensity):
    wave_real, wave_imag = illumination[0], illumination[1]
    saved = []
    for layer in range(SLICES):
        saved.append((wave_real, wave_imag))
        exit_real, exit_imag = complex_product(wave_real, wave_imag, illuminated_frame[layer, 0], illuminated_frame[layer, 1])
        if layer + 1 < SLICES:
            spec_real, spec_imag = forward_dft(exit_real, exit_imag)
            spec_real, spec_imag = complex_product(spec_real, spec_imag, filter_inphase, filter_quadrature)
            wave_real, wave_imag = inverse_dft(spec_real, spec_imag)
    far_real, far_imag = forward_dft(exit_real, exit_imag)
    misfit = far_real * far_real + far_imag * far_imag - observed_intensity
    back_real, back_imag = inverse_dft(misfit * far_real, misfit * far_imag)
    derivative_items = [None] * SLICES
    for layer in reversed(range(SLICES)):
        grad_real, grad_imag = conj_product(saved[layer][0], saved[layer][1], back_real, back_imag)
        derivative_items[layer] = jnp.stack([grad_real, grad_imag])
        head_real, head_imag = conj_product(illuminated_frame[layer, 0], illuminated_frame[layer, 1], back_real, back_imag)
        if layer > 0:
            spec_real, spec_imag = forward_dft(head_real, head_imag)
            spec_real, spec_imag = conj_product(filter_inphase, filter_quadrature, spec_real, spec_imag)
            back_real, back_imag = inverse_dft(spec_real, spec_imag)
    return jnp.stack(derivative_items), jnp.stack([head_real, head_imag])


def reference(specimen_transmit, illumination, fresnel_angle, recorded_intensity, frame_shifts):
    rows_total = specimen_transmit.shape[2]
    cols_total = specimen_transmit.shape[3]
    padded = jnp.pad(specimen_transmit, ((0, 0), (0, 0), (HALO, HALO), (HALO, HALO)), mode="wrap")
    filter_inphase = jnp.cos(fresnel_angle)
    filter_quadrature = jnp.sin(fresnel_angle)
    count = BRICKS_DOWN * BRICKS_ACROSS * SCAN_STOPS
    zero = jnp.zeros((), jnp.int32)

    def visit(carry, index):
        grad_pad, probe_sum = carry
        brick_down_number = index // (BRICKS_ACROSS * SCAN_STOPS)
        brick_across_number = (index // SCAN_STOPS) % BRICKS_ACROSS
        insert_frame = index % SCAN_STOPS
        shift = frame_shifts[brick_down_number, brick_across_number, insert_frame]
        start_row = (brick_down_number * TILE + shift[0] + HALO).astype(jnp.int32)
        start_col = (brick_across_number * TILE + shift[1] + HALO).astype(jnp.int32)
        illuminated_frame = lax.dynamic_slice(padded, (zero, zero, start_row, start_col), (SLICES, 2, FRAME_WIDTH, FRAME_WIDTH))
        derivative_items, incident_wave = location_derivative(illuminated_frame, illumination, filter_inphase, filter_quadrature, recorded_intensity[brick_down_number, brick_across_number, insert_frame])
        block = lax.dynamic_slice(grad_pad, (zero, zero, start_row, start_col), (SLICES, 2, FRAME_WIDTH, FRAME_WIDTH))
        grad_pad = lax.dynamic_update_slice(grad_pad, block + derivative_items, (zero, zero, start_row, start_col))
        return (grad_pad, probe_sum + incident_wave), None

    start = (jnp.zeros(padded.shape, specimen_transmit.dtype), jnp.zeros(illumination.shape, illumination.dtype))
    (grad_pad, probe_sum), _ = lax.scan(visit, start, jnp.arange(count, dtype=jnp.int32))
    core = grad_pad[:, :, HALO:HALO + rows_total, :]
    core = core.at[:, :, rows_total - HALO:, :].add(grad_pad[:, :, :HALO, :])
    core = core.at[:, :, :HALO, :].add(grad_pad[:, :, HALO + rows_total:, :])
    final = core[:, :, :, HALO:HALO + cols_total]
    final = final.at[:, :, :, cols_total - HALO:].add(core[:, :, :, :HALO])
    final = final.at[:, :, :, :HALO].add(core[:, :, :, HALO + cols_total:])
    return final, probe_sum
```

```python
import functools
import math

import jax
import jax.numpy as jnp
import ml_dtypes
import numpy as np
from jax import lax
from jax.experimental import pallas as pl
from jax.experimental.pallas import tpu as pltpu
from jax.sharding import PartitionSpec as P

HALO = 128
ROWS = 8
F32 = jnp.float32
BF16 = jnp.bfloat16


def make_tables(width):
    index = np.arange(width)
    angle = (index[:, None] * index[None, :] % width) * (2.0 * math.pi / width)
    both = np.concatenate([np.cos(angle), np.sin(angle)], axis=0) / math.sqrt(width)
    high = both.astype(ml_dtypes.bfloat16)
    low = (both - high.astype(np.float64)).astype(ml_dtypes.bfloat16)
    right = np.concatenate([high, high, low], axis=0)
    return jnp.asarray(right), jnp.asarray(np.ascontiguousarray(right.T))


def split_field(field):
    high = field.astype(BF16)
    low = (field - high.astype(F32)).astype(BF16)
    return high, low


def transform(real_part, imag_part, right, left, forward):
    width = real_part.shape[0]

    def arrange(r, i, axis):
        if forward:
            top = jnp.concatenate([r, i], axis=axis)
            bottom = jnp.concatenate([i, -r], axis=axis)
        else:
            top = jnp.concatenate([r, -i], axis=axis)
            bottom = jnp.concatenate([i, r], axis=axis)
        return jnp.concatenate([top, bottom], axis=1 - axis)

    rh, rl = split_field(real_part)
    ih, il = split_field(imag_part)
    high = arrange(rh, ih, 1)
    field = jnp.concatenate([high, arrange(rl, il, 1), high], axis=1)
    mid = jnp.dot(field, right[...], preferred_element_type=F32)
    rh, rl = split_field(mid[:width])
    ih, il = split_field(mid[width:])
    high = arrange(rh, ih, 0)
    field = jnp.concatenate([high, arrange(rl, il, 0), high], axis=0)
    out = jnp.dot(left[...], field, preferred_element_type=F32)
    return out[:, :width], out[:, width:]


def complex_product(a_real, a_imag, b_real, b_imag):
    return (a_real * b_real - a_imag * b_imag, a_real * b_imag + a_imag * b_real)


def conj_product(a_real, a_imag, b_real, b_imag):
    return (a_real * b_real + a_imag * b_imag, a_real * b_imag - a_imag * b_real)


def local_kernel(
    layers, shifts, mid, west, east, north, south, ncorn, scorn, illum, filt, seen, right, left,
    g_mid, g_west, g_east, g_north, g_south, g_ncorn, g_scorn, g_probe,
    ext, acc, win,
):
    tile = mid.shape[1]
    width = illum.shape[1]
    places = seen.shape[0]
    a, b = HALO, HALO + tile
    e = b + HALO
    parts = (
        (mid, slice(a, b), slice(a, b), None),
        (west, slice(a, b), slice(0, a), None),
        (east, slice(a, b), slice(b, e), None),
        (north, slice(0, a), slice(a, b), None),
        (south, slice(b, e), slice(a, b), None),
        (ncorn, slice(0, a), slice(0, a), 0),
        (ncorn, slice(0, a), slice(b, e), 1),
        (scorn, slice(b, e), slice(0, a), 0),
        (scorn, slice(b, e), slice(b, e), 1),
    )
    for ref, rows, cols, side in parts:
        ext[:, rows, cols] = ref[...] if side is None else ref[side]
    acc[...] = jnp.zeros_like(acc)
    g_probe[...] = jnp.zeros_like(g_probe)

    @pl.loop(0, places)
    def _(p):
        start_row = shifts[p, 0] + HALO
        start_col = shifts[p, 1] + HALO
        block = jnp.where(start_col > HALO, 1, 0)
        base = pl.multiple_of(block * HALO, HALO)
        rest = start_col - base
        span = width + HALO
        first = pl.multiple_of(start_row // ROWS * ROWS, ROWS)
        over = start_row - first
        tall = width + ROWS
        rows = pl.ds(first, tall)
        for c in range(2 * layers):
            wide = ext[c, rows, pl.ds(base, span)]
            wide = pltpu.roll(wide, lax.rem(tall - over, tall), 0)[:width]
            win[c] = pltpu.roll(wide, lax.rem(span - rest, span), 1)[:, :width]
        wave = (illum[0], illum[1])
        saved = []
        for layer in range(layers):
            saved.append(wave)
            out = complex_product(*wave, win[2 * layer], win[2 * layer + 1])
            if layer + 1 < layers:
                spec = transform(*out, right, left, True)
                spec = complex_product(*spec, filt[0], filt[1])
                wave = transform(*spec, right, left, False)
        far_real, far_imag = transform(*out, right, left, True)
        misfit = far_real * far_real + far_imag * far_imag - seen[p]
        back = transform(misfit * far_real, misfit * far_imag, right, left, False)
        for layer in reversed(range(layers)):
            grads = conj_product(*saved[layer], *back)
            for k in range(2):
                wide = jnp.concatenate([grads[k], jnp.zeros((width, HALO), F32)], axis=1)
                wide = pltpu.roll(wide, rest, 1)
                wide = jnp.concatenate([wide, jnp.zeros((ROWS, span), F32)], axis=0)
                wide = pltpu.roll(wide, over, 0)
                acc[2 * layer + k, rows, pl.ds(base, span)] += wide
            head = conj_product(win[2 * layer], win[2 * layer + 1], *back)
            if layer > 0:
                spec = transform(*head, right, left, True)
                spec = conj_product(filt[0], filt[1], *spec)
                back = transform(*spec, right, left, False)
        g_probe[0] += head[0]
        g_probe[1] += head[1]

    outs = (g_mid, g_west, g_east, g_north, g_south, g_ncorn, g_ncorn, g_scorn, g_scorn)
    for (_, rows, cols, side), out in zip(parts, outs):
        if side is None:
            out[...] = acc[:, rows, cols]
        else:
            out[side] = acc[:, rows, cols]


def local_gradients(layers, shifts, pieces, illum, filt, seen, right, left):
    chans, tile = pieces[0].shape[:2]
    width = illum.shape[1]
    side = tile + 2 * HALO
    vmem = pl.BlockSpec(memory_space=pltpu.VMEM)
    shapes = [x.shape for x in pieces] + [illum.shape]
    return pl.pallas_call(
        functools.partial(local_kernel, layers),
        out_shape=[jax.ShapeDtypeStruct(s, F32) for s in shapes],
        in_specs=[pl.BlockSpec(memory_space=pltpu.SMEM)] + [vmem] * 12,
        out_specs=[vmem] * 8,
        scratch_shapes=[
            pltpu.VMEM((chans, side + ROWS, side), F32),
            pltpu.VMEM((chans, side + ROWS, side), F32),
            pltpu.VMEM((chans, width, width), F32),
        ],
        compiler_params=pltpu.CompilerParams(vmem_limit_bytes=56 * 2**20),
        name="local_gradients",
    )(shifts, *pieces, illum, filt, seen, right, left)


def ring(axis):
    count = lax.axis_size(axis)
    up = [(i, (i + 1) % count) for i in range(count)]
    return up, [(t, s) for s, t in up]


def body(specimen_transmit, illumination, fresnel_angle, recorded_intensity, frame_shifts):
    layers = specimen_transmit.shape[0]
    tile = specimen_transmit.shape[2]
    width = illumination.shape[1]
    right, left = make_tables(width)
    filt = jnp.stack([jnp.cos(fresnel_angle), jnp.sin(fresnel_angle)])
    mid = specimen_transmit.reshape(2 * layers, tile, specimen_transmit.shape[3])
    row_up, row_down = ring("row")
    col_up, col_down = ring("col")
    west = lax.ppermute(mid[:, :, -HALO:], "col", col_up)
    east = lax.ppermute(mid[:, :, :HALO], "col", col_down)
    north = lax.ppermute(mid[:, -HALO:], "row", row_up)
    south = lax.ppermute(mid[:, :HALO], "row", row_down)
    sides = jnp.stack([west, east])
    ncorn = lax.ppermute(sides[:, :, -HALO:], "row", row_up)
    scorn = lax.ppermute(sides[:, :, :HALO], "row", row_down)
    pieces = (mid, west, east, north, south, ncorn, scorn)
    g_mid, g_west, g_east, g_north, g_south, g_ncorn, g_scorn, g_probe = local_gradients(
        layers, frame_shifts[0, 0], pieces, illumination, filt, recorded_intensity[0, 0], right, left
    )
    from_south = lax.ppermute(g_ncorn, "row", row_down)
    from_north = lax.ppermute(g_scorn, "row", row_up)
    mid_south = lax.ppermute(g_north, "row", row_down)
    mid_north = lax.ppermute(g_south, "row", row_up)
    sides = jnp.stack([g_west, g_east])
    sides = sides.at[:, :, -HALO:].add(from_south)
    sides = sides.at[:, :, :HALO].add(from_north)
    from_east = lax.ppermute(sides[0], "col", col_down)
    from_west = lax.ppermute(sides[1], "col", col_up)
    far = tile - HALO

    def fit(x, low_row, low_col):
        rows, cols = x.shape[1:]
        pads = ((0, 0), (low_row, tile - rows - low_row), (low_col, tile - cols - low_col))
        return jnp.pad(x, pads)

    result = (
        g_mid
        + fit(mid_south, far, 0)
        + fit(mid_north, 0, 0)
        + fit(from_east, 0, far)
        + fit(from_west, 0, 0)
    )
    result = result.reshape(specimen_transmit.shape)
    partial_rows = lax.psum_scatter(g_probe, "row", scatter_dimension=1, tiled=True)
    probe_part = lax.psum_scatter(partial_rows, "col", scatter_dimension=2, tiled=True)
    return (result, probe_part)


def solution(mesh):
    placed = (
        P(None, None, "row", "col"),
        P(),
        P(),
        P("row", "col", None, None, None),
        P("row", "col", None, None),
    )
    return jax.shard_map(
        body,
        mesh=mesh,
        in_specs=placed,
        out_specs=(P(None, None, "row", "col"), P(None, "row", "col")),
        check_vma=False,
    )
```

```python
import functools
import math

import jax
import jax.numpy as jnp
import ml_dtypes
import numpy as np
from jax import lax
from jax.experimental import pallas as pl
from jax.experimental.pallas import tpu as pltpu
from jax.sharding import PartitionSpec as P

HALO = 128
ROWS = 8
F32 = jnp.float32
BF16 = jnp.bfloat16


def make_tables(width):
    index = np.arange(width)
    angle = (index[:, None] * index[None, :] % width) * (2.0 * math.pi / width)
    both = np.concatenate([np.cos(angle), np.sin(angle)], axis=0) / math.sqrt(width)
    high = both.astype(ml_dtypes.bfloat16)
    low = (both - high.astype(np.float64)).astype(ml_dtypes.bfloat16)
    right = np.concatenate([high, high, low], axis=0)
    return jnp.asarray(right), jnp.asarray(np.ascontiguousarray(right.T))


def split_field(field):
    high = field.astype(BF16)
    low = (field - high.astype(F32)).astype(BF16)
    return high, low


def transform(real_part, imag_part, right, left, forward):
    width = real_part.shape[0]

    def arrange(r, i, axis):
        if forward:
            top = jnp.concatenate([r, i], axis=axis)
            bottom = jnp.concatenate([i, -r], axis=axis)
        else:
            top = jnp.concatenate([r, -i], axis=axis)
            bottom = jnp.concatenate([i, r], axis=axis)
        return jnp.concatenate([top, bottom], axis=1 - axis)

    rh, rl = split_field(real_part)
    ih, il = split_field(imag_part)
    high = arrange(rh, ih, 1)
    field = jnp.concatenate([high, arrange(rl, il, 1), high], axis=1)
    mid = jnp.dot(field, right[...], preferred_element_type=F32)
    rh, rl = split_field(mid[:width])
    ih, il = split_field(mid[width:])
    high = arrange(rh, ih, 0)
    field = jnp.concatenate([high, arrange(rl, il, 0), high], axis=0)
    out = jnp.dot(left[...], field, preferred_element_type=F32)
    return out[:, :width], out[:, width:]


def complex_product(a_real, a_imag, b_real, b_imag):
    return (a_real * b_real - a_imag * b_imag, a_real * b_imag + a_imag * b_real)


def conj_product(a_real, a_imag, b_real, b_imag):
    return (a_real * b_real + a_imag * b_imag, a_real * b_imag - a_imag * b_real)


def local_kernel(
    layers, shifts, mid, west, east, north, south, ncorn, scorn, illum, filt, seen, right, left,
    g_mid, g_west, g_east, g_north, g_south, g_ncorn, g_scorn, g_probe,
    ext, acc, win,
):
    tile = mid.shape[1]
    width = illum.shape[1]
    places = seen.shape[0]
    a, b = HALO, HALO + tile
    e = b + HALO
    parts = (
        (mid, slice(a, b), slice(a, b), None),
        (west, slice(a, b), slice(0, a), None),
        (east, slice(a, b), slice(b, e), None),
        (north, slice(0, a), slice(a, b), None),
        (south, slice(b, e), slice(a, b), None),
        (ncorn, slice(0, a), slice(0, a), 0),
        (ncorn, slice(0, a), slice(b, e), 1),
        (scorn, slice(b, e), slice(0, a), 0),
        (scorn, slice(b, e), slice(b, e), 1),
    )
    for ref, rows, cols, side in parts:
        ext[:, rows, cols] = ref[...] if side is None else ref[side]
    acc[...] = jnp.zeros_like(acc)
    g_probe[...] = jnp.zeros_like(g_probe)

    @pl.loop(0, places)
    def _(p):
        start_row = shifts[p, 0] + HALO
        start_col = shifts[p, 1] + HALO
        block = jnp.where(start_col > HALO, 1, 0)
        base = pl.multiple_of(block * HALO, HALO)
        rest = start_col - base
        span = width + HALO
        first = pl.multiple_of(start_row // ROWS * ROWS, ROWS)
        over = start_row - first
        tall = width + ROWS
        rows = pl.ds(first, tall)
        for c in range(2 * layers):
            wide = ext[c, rows, pl.ds(base, span)]
            wide = pltpu.roll(wide, lax.rem(tall - over, tall), 0)[:width]
            win[c] = pltpu.roll(wide, lax.rem(span - rest, span), 1)[:, :width]
        wave = (illum[0], illum[1])
        saved = []
        for layer in range(layers):
            saved.append(wave)
            out = complex_product(*wave, win[2 * layer], win[2 * layer + 1])
            if layer + 1 < layers:
                spec = transform(*out, right, left, True)
                spec = complex_product(*spec, filt[0], filt[1])
                wave = transform(*spec, right, left, False)
        far_real, far_imag = transform(*out, right, left, True)
        misfit = far_real * far_real + far_imag * far_imag - seen[p]
        back = transform(misfit * far_real, misfit * far_imag, right, left, False)
        for layer in reversed(range(layers)):
            grads = conj_product(*saved[layer], *back)
            for k in range(2):
                wide = jnp.concatenate([grads[k], jnp.zeros((width, HALO), F32)], axis=1)
                wide = pltpu.roll(wide, rest, 1)
                wide = jnp.concatenate([wide, jnp.zeros((ROWS, span), F32)], axis=0)
                wide = pltpu.roll(wide, over, 0)
                acc[2 * layer + k, rows, pl.ds(base, span)] += wide
            head = conj_product(win[2 * layer], win[2 * layer + 1], *back)
            if layer > 0:
                spec = transform(*head, right, left, True)
                spec = conj_product(filt[0], filt[1], *spec)
                back = transform(*spec, right, left, False)
        g_probe[0] += head[0]
        g_probe[1] += head[1]

    outs = (g_mid, g_west, g_east, g_north, g_south, g_ncorn, g_ncorn, g_scorn, g_scorn)
    for (_, rows, cols, side), out in zip(parts, outs):
        if side is None:
            out[...] = acc[:, rows, cols]
        else:
            out[side] = acc[:, rows, cols]


def local_gradients(layers, shifts, pieces, illum, filt, seen, right, left):
    chans, tile = pieces[0].shape[:2]
    width = illum.shape[1]
    side = tile + 2 * HALO
    vmem = pl.BlockSpec(memory_space=pltpu.VMEM)
    shapes = [x.shape for x in pieces] + [illum.shape]
    return pl.pallas_call(
        functools.partial(local_kernel, layers),
        out_shape=[jax.ShapeDtypeStruct(s, F32) for s in shapes],
        in_specs=[pl.BlockSpec(memory_space=pltpu.SMEM)] + [vmem] * 12,
        out_specs=[vmem] * 8,
        scratch_shapes=[
            pltpu.VMEM((chans, side + ROWS, side), F32),
            pltpu.VMEM((chans, side + ROWS, side), F32),
            pltpu.VMEM((chans, width, width), F32),
        ],
        compiler_params=pltpu.CompilerParams(vmem_limit_bytes=56 * 2**20),
        name="local_gradients",
    )(shifts, *pieces, illum, filt, seen, right, left)


def remote(src, dst, sems, slot, device):
    return pltpu.make_async_remote_copy(
        src_ref=src,
        dst_ref=dst,
        send_sem=sems.at[0, slot],
        recv_sem=sems.at[1, slot],
        device_id=device,
        device_id_type=pl.DeviceIdType.MESH,
    )


def greet(peers):
    barrier = pltpu.get_barrier_semaphore()
    for device in peers:
        pl.semaphore_signal(barrier, inc=1, device_id=device, device_id_type=pl.DeviceIdType.MESH)
    pl.semaphore_wait(barrier, len(peers))


def halo_kernel(layers, count, across, mid, west, east, north, south, ncorn, scorn, sems):
    tile_rows, tile_cols = mid.shape[1:]
    row, col = lax.axis_index("row"), lax.axis_index("col")
    below = (lax.rem(row + 1, count), col)
    above = (lax.rem(row + count - 1, count), col)
    toeast = (row, lax.rem(col + 1, across))
    towest = (row, lax.rem(col + across - 1, across))
    greet([below, above, toeast, towest])
    last_rows = pl.ds(tile_rows - HALO, HALO)
    first_rows = pl.ds(0, HALO)
    last_cols = pl.ds(tile_cols - HALO, HALO)
    first_cols = pl.ds(0, HALO)
    sides, rows, corners = [], [], []
    for l in range(layers):
        ch = pl.ds(2 * l, 2)
        slot = 8 * l
        sides.append((
            remote(mid.at[ch, :, last_cols], west.at[ch], sems, slot, toeast),
            remote(mid.at[ch, :, first_cols], east.at[ch], sems, slot + 1, towest),
        ))
        rows.append(remote(mid.at[ch, last_rows], north.at[ch], sems, slot + 2, below))
        rows.append(remote(mid.at[ch, first_rows], south.at[ch], sems, slot + 3, above))
        for k, ref in enumerate((west, east)):
            corners.append((
                remote(ref.at[ch, last_rows], ncorn.at[k, ch], sems, slot + 4 + k, below),
                remote(ref.at[ch, first_rows], scorn.at[k, ch], sems, slot + 6 + k, above),
            ))
    for pair in sides:
        for copy in pair:
            copy.start()
    for copy in rows:
        copy.start()
    for l in range(layers):
        for k in range(2):
            sides[l][k].wait_recv()
            for copy in corners[2 * l + k]:
                copy.start()
    for copy in rows:
        copy.wait()
    for pair in corners:
        for copy in pair:
            copy.wait()
    for pair in sides:
        for copy in pair:
            copy.wait_send()


def fetch_halo(layers, mid):
    count, across = lax.axis_size("row"), lax.axis_size("col")
    chans, tile_rows, tile_cols = mid.shape
    side = (chans, tile_rows, HALO)
    flat = (chans, HALO, tile_cols)
    corner = (2, chans, HALO, HALO)
    vmem = pl.BlockSpec(memory_space=pltpu.VMEM)
    return pl.pallas_call(
        functools.partial(halo_kernel, layers, count, across),
        out_shape=[jax.ShapeDtypeStruct(s, F32) for s in (side, side, flat, flat, corner, corner)],
        in_specs=[vmem],
        out_specs=[vmem] * 6,
        scratch_shapes=[pltpu.SemaphoreType.DMA((2, 8 * layers))],
        compiler_params=pltpu.CompilerParams(
            collective_id=0, has_side_effects=True, vmem_limit_bytes=24 * 2**20
        ),
        name="fetch_halo",
    )(mid)


def settle_kernel(
    layers, count, across,
    g_mid, g_west, g_east, g_north, g_south, g_ncorn, g_scorn, g_probe, out, probe,
    south_corn, north_corn, side_send, side_recv, south_mid, north_mid,
    probe_rows, probe_send, probe_cols, sems, row_sems, col_sems,
):
    tile_rows, tile_cols = out.shape[1:]
    row, col = lax.axis_index("row"), lax.axis_index("col")
    row_peers = [(lax.rem(row + d, count), col) for d in range(1, count)]
    col_peers = [(row, lax.rem(col + d, across)) for d in range(1, across)]
    below, above = row_peers[0], row_peers[-1]
    toeast, towest = col_peers[0], col_peers[-1]
    greet(row_peers + col_peers)
    last_rows = pl.ds(tile_rows - HALO, HALO)
    first_rows = pl.ds(0, HALO)
    corners, mids = [], []
    for l in reversed(range(layers)):
        ch = pl.ds(2 * l, 2)
        slot = 8 * l
        for k in range(2):
            corners.append((l, k, (
                remote(g_ncorn.at[k, ch], south_corn.at[k, ch], sems, slot + k, above),
                remote(g_scorn.at[k, ch], north_corn.at[k, ch], sems, slot + 2 + k, below),
            )))
        mids.append((l, (
            remote(g_north.at[ch], south_mid.at[ch], sems, slot + 4, above),
            remote(g_south.at[ch], north_mid.at[ch], sems, slot + 5, below),
        )))
    for _, _, pair in corners:
        for copy in pair:
            copy.start()
    strip = probe.shape[1]
    row_copies = []
    for d in range(1, count):
        device = row_peers[d - 1]
        part = pl.ds(pl.multiple_of(device[0] * strip, strip), strip)
        copy = remote(g_probe.at[:, part], probe_rows.at[d - 1], row_sems, d - 1, device)
        copy.start()
        row_copies.append(copy)
    for _, pair in mids:
        for copy in pair:
            copy.start()
    sides = []
    for l, k, pair in corners:
        ch = pl.ds(2 * l, 2)
        for copy in pair:
            copy.wait_recv()
        side_send[k, ch] = (g_west, g_east)[k][ch]
        side_send[k, ch, last_rows] += south_corn[k, ch]
        side_send[k, ch, first_rows] += north_corn[k, ch]
        copy = remote(
            side_send.at[k, ch], side_recv.at[k, ch], sems, 8 * l + 6 + k, (towest, toeast)[k]
        )
        copy.start()
        sides.append((l, k, copy))
    total = g_probe[:, pl.ds(pl.multiple_of(row * strip, strip), strip)]
    for d, copy in enumerate(row_copies):
        copy.wait_recv()
        total += probe_rows[d]
    narrow = probe.shape[2]
    for c in range(across):
        probe_send[c] = total[:, :, c * narrow : (c + 1) * narrow]
    col_copies = []
    for d in range(1, across):
        device = col_peers[d - 1]
        copy = remote(probe_send.at[device[1]], probe_cols.at[d - 1], col_sems, d - 1, device)
        copy.start()
        col_copies.append(copy)
    out[...] = g_mid[...]
    for l, pair in mids:
        ch = pl.ds(2 * l, 2)
        for copy in pair:
            copy.wait_recv()
        out[ch, last_rows] += south_mid[ch]
        out[ch, first_rows] += north_mid[ch]
    for l, k, copy in sides:
        ch = pl.ds(2 * l, 2)
        cols = pl.ds((tile_cols - HALO) * (1 - k), HALO)
        copy.wait_recv()
        out[ch, :, cols] += side_recv[k, ch]
    part = probe_send[col]
    for d, copy in enumerate(col_copies):
        copy.wait_recv()
        part += probe_cols[d]
    probe[...] = part
    for _, _, pair in corners:
        for copy in pair:
            copy.wait_send()
    for _, pair in mids:
        for copy in pair:
            copy.wait_send()
    for _, _, copy in sides:
        copy.wait_send()
    for copy in row_copies + col_copies:
        copy.wait_send()


def settle(layers, grads):
    count, across = lax.axis_size("row"), lax.axis_size("col")
    chans, tile_rows, tile_cols = grads[0].shape
    width = grads[7].shape[1]
    strip, narrow = width // count, width // across
    vmem = pl.BlockSpec(memory_space=pltpu.VMEM)
    dma = pltpu.SemaphoreType.DMA
    return pl.pallas_call(
        functools.partial(settle_kernel, layers, count, across),
        out_shape=[
            jax.ShapeDtypeStruct((chans, tile_rows, tile_cols), F32),
            jax.ShapeDtypeStruct((2, strip, narrow), F32),
        ],
        in_specs=[vmem] * 8,
        out_specs=[vmem] * 2,
        scratch_shapes=[
            pltpu.VMEM((2, chans, HALO, HALO), F32),
            pltpu.VMEM((2, chans, HALO, HALO), F32),
            pltpu.VMEM((2, chans, tile_rows, HALO), F32),
            pltpu.VMEM((2, chans, tile_rows, HALO), F32),
            pltpu.VMEM((chans, HALO, tile_cols), F32),
            pltpu.VMEM((chans, HALO, tile_cols), F32),
            pltpu.VMEM((count - 1, 2, strip, width), F32),
            pltpu.VMEM((across, 2, strip, narrow), F32),
            pltpu.VMEM((across - 1, 2, strip, narrow), F32),
            dma((2, 8 * layers)),
            dma((2, count - 1)),
            dma((2, across - 1)),
        ],
        compiler_params=pltpu.CompilerParams(
            collective_id=1, has_side_effects=True, vmem_limit_bytes=40 * 2**20
        ),
        name="settle_gradients",
    )(*grads)


def body(specimen_transmit, illumination, fresnel_angle, recorded_intensity, frame_shifts):
    layers = specimen_transmit.shape[0]
    tile = specimen_transmit.shape[2]
    width = illumination.shape[1]
    right, left = make_tables(width)
    filt = jnp.stack([jnp.cos(fresnel_angle), jnp.sin(fresnel_angle)])
    mid = specimen_transmit.reshape(2 * layers, tile, specimen_transmit.shape[3])
    pieces = (mid, *fetch_halo(layers, mid))
    grads = local_gradients(
        layers, frame_shifts[0, 0], pieces, illumination, filt, recorded_intensity[0, 0], right, left
    )
    result, probe_part = settle(layers, grads)
    return (result.reshape(specimen_transmit.shape), probe_part)


def solution(mesh):
    placed = (
        P(None, None, "row", "col"),
        P(),
        P(),
        P("row", "col", None, None, None),
        P("row", "col", None, None),
    )
    return jax.shard_map(
        body,
        mesh=mesh,
        in_specs=placed,
        out_specs=(P(None, None, "row", "col"), P(None, "row", "col")),
        check_vma=False,
    )
```

```python
import functools
import math

import jax
import jax.numpy as jnp
import ml_dtypes
import numpy as np
from jax import lax
from jax.experimental import pallas as pl
from jax.experimental.pallas import tpu as pltpu
from jax.sharding import PartitionSpec as P

HALO = 128
ROWS = 8
F32 = jnp.float32
BF16 = jnp.bfloat16


def make_tables(width):
    index = np.arange(width)
    angle = (index[:, None] * index[None, :] % width) * (2.0 * math.pi / width)
    both = np.concatenate([np.cos(angle), np.sin(angle)], axis=0) / math.sqrt(width)
    high = both.astype(ml_dtypes.bfloat16)
    low = (both - high.astype(np.float64)).astype(ml_dtypes.bfloat16)
    right = np.concatenate([high, high, low], axis=0)
    return jnp.asarray(right), jnp.asarray(np.ascontiguousarray(right.T))


def split_field(field):
    high = field.astype(BF16)
    low = (field - high.astype(F32)).astype(BF16)
    return high, low


def transform(real_part, imag_part, right, left, forward):
    width = real_part.shape[0]

    def arrange(r, i, axis):
        if forward:
            top = jnp.concatenate([r, i], axis=axis)
            bottom = jnp.concatenate([i, -r], axis=axis)
        else:
            top = jnp.concatenate([r, -i], axis=axis)
            bottom = jnp.concatenate([i, r], axis=axis)
        return jnp.concatenate([top, bottom], axis=1 - axis)

    rh, rl = split_field(real_part)
    ih, il = split_field(imag_part)
    high = arrange(rh, ih, 1)
    field = jnp.concatenate([high, arrange(rl, il, 1), high], axis=1)
    mid = jnp.dot(field, right[...], preferred_element_type=F32)
    rh, rl = split_field(mid[:width])
    ih, il = split_field(mid[width:])
    high = arrange(rh, ih, 0)
    field = jnp.concatenate([high, arrange(rl, il, 0), high], axis=0)
    out = jnp.dot(left[...], field, preferred_element_type=F32)
    return out[:, :width], out[:, width:]


def complex_product(a_real, a_imag, b_real, b_imag):
    return (a_real * b_real - a_imag * b_imag, a_real * b_imag + a_imag * b_real)


def conj_product(a_real, a_imag, b_real, b_imag):
    return (a_real * b_real + a_imag * b_imag, a_real * b_imag - a_imag * b_real)


def local_kernel(
    layers, shifts, mid, west, east, north, south, ncorn, scorn, illum, filt, seen, right, left,
    g_mid, g_west, g_east, g_north, g_south, g_ncorn, g_scorn, g_probe,
    ext, acc, win,
):
    tile = mid.shape[1]
    width = illum.shape[1]
    places = seen.shape[0]
    a, b = HALO, HALO + tile
    e = b + HALO
    parts = (
        (mid, slice(a, b), slice(a, b), None),
        (west, slice(a, b), slice(0, a), None),
        (east, slice(a, b), slice(b, e), None),
        (north, slice(0, a), slice(a, b), None),
        (south, slice(b, e), slice(a, b), None),
        (ncorn, slice(0, a), slice(0, a), 0),
        (ncorn, slice(0, a), slice(b, e), 1),
        (scorn, slice(b, e), slice(0, a), 0),
        (scorn, slice(b, e), slice(b, e), 1),
    )
    for ref, rows, cols, side in parts:
        ext[:, rows, cols] = ref[...] if side is None else ref[side]
    acc[...] = jnp.zeros_like(acc)
    g_probe[...] = jnp.zeros_like(g_probe)

    @pl.loop(0, places)
    def _(p):
        start_row = shifts[p, 0] + HALO
        start_col = shifts[p, 1] + HALO
        block = jnp.where(start_col > HALO, 1, 0)
        base = pl.multiple_of(block * HALO, HALO)
        rest = start_col - base
        span = width + HALO
        first = pl.multiple_of(start_row // ROWS * ROWS, ROWS)
        over = start_row - first
        tall = width + ROWS
        rows = pl.ds(first, tall)
        for c in range(2 * layers):
            wide = ext[c, rows, pl.ds(base, span)]
            wide = pltpu.roll(wide, lax.rem(tall - over, tall), 0)[:width]
            win[c] = pltpu.roll(wide, lax.rem(span - rest, span), 1)[:, :width]
        wave = (illum[0], illum[1])
        saved = []
        for layer in range(layers):
            saved.append(wave)
            out = complex_product(*wave, win[2 * layer], win[2 * layer + 1])
            if layer + 1 < layers:
                spec = transform(*out, right, left, True)
                spec = complex_product(*spec, filt[0], filt[1])
                wave = transform(*spec, right, left, False)
        far_real, far_imag = transform(*out, right, left, True)
        misfit = far_real * far_real + far_imag * far_imag - seen[p]
        back = transform(misfit * far_real, misfit * far_imag, right, left, False)
        for layer in reversed(range(layers)):
            grads = conj_product(*saved[layer], *back)
            for k in range(2):
                wide = jnp.concatenate([grads[k], jnp.zeros((width, HALO), F32)], axis=1)
                wide = pltpu.roll(wide, rest, 1)
                wide = jnp.concatenate([wide, jnp.zeros((ROWS, span), F32)], axis=0)
                wide = pltpu.roll(wide, over, 0)
                acc[2 * layer + k, rows, pl.ds(base, span)] += wide
            head = conj_product(win[2 * layer], win[2 * layer + 1], *back)
            if layer > 0:
                spec = transform(*head, right, left, True)
                spec = conj_product(filt[0], filt[1], *spec)
                back = transform(*spec, right, left, False)
        g_probe[0] += head[0]
        g_probe[1] += head[1]

    outs = (g_mid, g_west, g_east, g_north, g_south, g_ncorn, g_ncorn, g_scorn, g_scorn)
    for (_, rows, cols, side), out in zip(parts, outs):
        if side is None:
            out[...] = acc[:, rows, cols]
        else:
            out[side] = acc[:, rows, cols]


def local_gradients(layers, shifts, pieces, illum, filt, seen, right, left):
    chans, tile = pieces[0].shape[:2]
    width = illum.shape[1]
    side = tile + 2 * HALO
    vmem = pl.BlockSpec(memory_space=pltpu.VMEM)
    shapes = [x.shape for x in pieces] + [illum.shape]
    return pl.pallas_call(
        functools.partial(local_kernel, layers),
        out_shape=[jax.ShapeDtypeStruct(s, F32) for s in shapes],
        in_specs=[pl.BlockSpec(memory_space=pltpu.SMEM)] + [vmem] * 12,
        out_specs=[vmem] * 8,
        scratch_shapes=[
            pltpu.VMEM((chans, side + ROWS, side), F32),
            pltpu.VMEM((chans, side + ROWS, side), F32),
            pltpu.VMEM((chans, width, width), F32),
        ],
        compiler_params=pltpu.CompilerParams(vmem_limit_bytes=34 * 2**20),
        name="local_gradients",
    )(shifts, *pieces, illum, filt, seen, right, left)


def remote(src, dst, sems, slot, device):
    return pltpu.make_async_remote_copy(
        src_ref=src,
        dst_ref=dst,
        send_sem=sems.at[0, slot],
        recv_sem=sems.at[1, slot],
        device_id=device,
        device_id_type=pl.DeviceIdType.MESH,
    )


def greet(peers):
    barrier = pltpu.get_barrier_semaphore()
    for device in peers:
        pl.semaphore_signal(barrier, inc=1, device_id=device, device_id_type=pl.DeviceIdType.MESH)
    pl.semaphore_wait(barrier, len(peers))


def halo_kernel(
    layers, count, across, mid, angle, west, east, north, south, ncorn, scorn, filt, sems
):
    tile_rows, tile_cols = mid.shape[1:]
    row, col = lax.axis_index("row"), lax.axis_index("col")
    below = (lax.rem(row + 1, count), col)
    above = (lax.rem(row + count - 1, count), col)
    toeast = (row, lax.rem(col + 1, across))
    towest = (row, lax.rem(col + across - 1, across))
    greet([below, above, toeast, towest])
    last_rows = pl.ds(tile_rows - HALO, HALO)
    first_rows = pl.ds(0, HALO)
    last_cols = pl.ds(tile_cols - HALO, HALO)
    first_cols = pl.ds(0, HALO)
    sides, rows, corners = [], [], []
    for l in range(layers):
        ch = pl.ds(2 * l, 2)
        slot = 8 * l
        sides.append((
            remote(mid.at[ch, :, last_cols], west.at[ch], sems, slot, toeast),
            remote(mid.at[ch, :, first_cols], east.at[ch], sems, slot + 1, towest),
        ))
        rows.append(remote(mid.at[ch, last_rows], north.at[ch], sems, slot + 2, below))
        rows.append(remote(mid.at[ch, first_rows], south.at[ch], sems, slot + 3, above))
        for k, ref in enumerate((west, east)):
            corners.append((
                remote(ref.at[ch, last_rows], ncorn.at[k, ch], sems, slot + 4 + k, below),
                remote(ref.at[ch, first_rows], scorn.at[k, ch], sems, slot + 6 + k, above),
            ))
    for pair in sides:
        for copy in pair:
            copy.start()
    for copy in rows:
        copy.start()
    filt[0] = jnp.cos(angle[...])
    filt[1] = jnp.sin(angle[...])
    for l in range(layers):
        for k in range(2):
            sides[l][k].wait_recv()
            for copy in corners[2 * l + k]:
                copy.start()
    for copy in rows:
        copy.wait()
    for pair in corners:
        for copy in pair:
            copy.wait()
    for pair in sides:
        for copy in pair:
            copy.wait_send()


def fetch_halo(layers, mid, angle):
    count, across = lax.axis_size("row"), lax.axis_size("col")
    chans, tile_rows, tile_cols = mid.shape
    side = (chans, tile_rows, HALO)
    flat = (chans, HALO, tile_cols)
    corner = (2, chans, HALO, HALO)
    vmem = pl.BlockSpec(memory_space=pltpu.VMEM)
    return pl.pallas_call(
        functools.partial(halo_kernel, layers, count, across),
        out_shape=[
            jax.ShapeDtypeStruct(s, F32)
            for s in (side, side, flat, flat, corner, corner, (2, *angle.shape))
        ],
        in_specs=[vmem] * 2,
        out_specs=[vmem] * 7,
        scratch_shapes=[pltpu.SemaphoreType.DMA((2, 8 * layers))],
        compiler_params=pltpu.CompilerParams(
            collective_id=0, has_side_effects=True, vmem_limit_bytes=24 * 2**20
        ),
        name="fetch_halo",
    )(mid, angle)


def settle_kernel(
    layers, count, across,
    g_mid, g_west, g_east, g_north, g_south, g_ncorn, g_scorn, g_probe, out, probe,
    south_corn, north_corn, side_send, side_recv, south_mid, north_mid,
    probe_rows, probe_send, probe_cols, sems, row_sems, col_sems,
):
    tile_rows, tile_cols = out.shape[1:]
    row, col = lax.axis_index("row"), lax.axis_index("col")
    row_peers = [(lax.rem(row + d, count), col) for d in range(1, count)]
    col_peers = [(row, lax.rem(col + d, across)) for d in range(1, across)]
    below, above = row_peers[0], row_peers[-1]
    toeast, towest = col_peers[0], col_peers[-1]
    greet(row_peers + col_peers)
    last_rows = pl.ds(tile_rows - HALO, HALO)
    first_rows = pl.ds(0, HALO)
    corners, mids = [], []
    for l in reversed(range(layers)):
        ch = pl.ds(2 * l, 2)
        slot = 8 * l
        for k in range(2):
            corners.append((l, k, (
                remote(g_ncorn.at[k, ch], south_corn.at[k, ch], sems, slot + k, above),
                remote(g_scorn.at[k, ch], north_corn.at[k, ch], sems, slot + 2 + k, below),
            )))
        mids.append((l, (
            remote(g_north.at[ch], south_mid.at[ch], sems, slot + 4, above),
            remote(g_south.at[ch], north_mid.at[ch], sems, slot + 5, below),
        )))
    for _, _, pair in corners:
        for copy in pair:
            copy.start()
    strip = probe.shape[1]
    row_copies = []
    for d in range(1, count):
        device = row_peers[d - 1]
        part = pl.ds(pl.multiple_of(device[0] * strip, strip), strip)
        copy = remote(g_probe.at[:, part], probe_rows.at[d - 1], row_sems, d - 1, device)
        copy.start()
        row_copies.append(copy)
    for _, pair in mids:
        for copy in pair:
            copy.start()
    sides = []
    for l, k, pair in corners:
        ch = pl.ds(2 * l, 2)
        for copy in pair:
            copy.wait_recv()
        side_send[k, ch] = (g_west, g_east)[k][ch]
        side_send[k, ch, last_rows] += south_corn[k, ch]
        side_send[k, ch, first_rows] += north_corn[k, ch]
        copy = remote(
            side_send.at[k, ch], side_recv.at[k, ch], sems, 8 * l + 6 + k, (towest, toeast)[k]
        )
        copy.start()
        sides.append((l, k, copy))
    total = g_probe[:, pl.ds(pl.multiple_of(row * strip, strip), strip)]
    for d, copy in enumerate(row_copies):
        copy.wait_recv()
        total += probe_rows[d]
    narrow = probe.shape[2]
    for c in range(across):
        probe_send[c] = total[:, :, c * narrow : (c + 1) * narrow]
    col_copies = []
    for d in range(1, across):
        device = col_peers[d - 1]
        copy = remote(probe_send.at[device[1]], probe_cols.at[d - 1], col_sems, d - 1, device)
        copy.start()
        col_copies.append(copy)
    out[...] = g_mid[...]
    for l, pair in mids:
        ch = pl.ds(2 * l, 2)
        for copy in pair:
            copy.wait_recv()
        out[ch, last_rows] += south_mid[ch]
        out[ch, first_rows] += north_mid[ch]
    for l, k, copy in sides:
        ch = pl.ds(2 * l, 2)
        cols = pl.ds((tile_cols - HALO) * (1 - k), HALO)
        copy.wait_recv()
        out[ch, :, cols] += side_recv[k, ch]
    part = probe_send[col]
    for d, copy in enumerate(col_copies):
        copy.wait_recv()
        part += probe_cols[d]
    probe[...] = part
    for _, _, pair in corners:
        for copy in pair:
            copy.wait_send()
    for _, pair in mids:
        for copy in pair:
            copy.wait_send()
    for _, _, copy in sides:
        copy.wait_send()
    for copy in row_copies + col_copies:
        copy.wait_send()


def settle(layers, grads):
    count, across = lax.axis_size("row"), lax.axis_size("col")
    chans, tile_rows, tile_cols = grads[0].shape
    width = grads[7].shape[1]
    strip, narrow = width // count, width // across
    vmem = pl.BlockSpec(memory_space=pltpu.VMEM)
    dma = pltpu.SemaphoreType.DMA
    return pl.pallas_call(
        functools.partial(settle_kernel, layers, count, across),
        out_shape=[
            jax.ShapeDtypeStruct((chans, tile_rows, tile_cols), F32),
            jax.ShapeDtypeStruct((2, strip, narrow), F32),
        ],
        in_specs=[vmem] * 8,
        out_specs=[vmem] * 2,
        scratch_shapes=[
            pltpu.VMEM((2, chans, HALO, HALO), F32),
            pltpu.VMEM((2, chans, HALO, HALO), F32),
            pltpu.VMEM((2, chans, tile_rows, HALO), F32),
            pltpu.VMEM((2, chans, tile_rows, HALO), F32),
            pltpu.VMEM((chans, HALO, tile_cols), F32),
            pltpu.VMEM((chans, HALO, tile_cols), F32),
            pltpu.VMEM((count - 1, 2, strip, width), F32),
            pltpu.VMEM((across, 2, strip, narrow), F32),
            pltpu.VMEM((across - 1, 2, strip, narrow), F32),
            dma((2, 8 * layers)),
            dma((2, count - 1)),
            dma((2, across - 1)),
        ],
        compiler_params=pltpu.CompilerParams(
            collective_id=1, has_side_effects=True, vmem_limit_bytes=30 * 2**20
        ),
        name="settle_gradients",
    )(*grads)


def body(specimen_transmit, illumination, fresnel_angle, recorded_intensity, frame_shifts):
    layers = specimen_transmit.shape[0]
    tile = specimen_transmit.shape[2]
    width = illumination.shape[1]
    right, left = make_tables(width)
    mid = specimen_transmit.reshape(2 * layers, tile, specimen_transmit.shape[3])
    *halo, filt = fetch_halo(layers, mid, fresnel_angle)
    pieces = (mid, *halo)
    grads = local_gradients(
        layers, frame_shifts[0, 0], pieces, illumination, filt, recorded_intensity[0, 0], right, left
    )
    result, probe_part = settle(layers, grads)
    return (result.reshape(specimen_transmit.shape), probe_part)


def solution(mesh):
    placed = (
        P(None, None, "row", "col"),
        P(),
        P(),
        P("row", "col", None, None, None),
        P("row", "col", None, None),
    )
    return jax.shard_map(
        body,
        mesh=mesh,
        in_specs=placed,
        out_specs=(P(None, None, "row", "col"), P(None, "row", "col")),
        check_vma=False,
    )
```

```python
import functools
import math

import jax
import jax.numpy as jnp
import ml_dtypes
import numpy as np
from jax import lax
from jax.experimental import pallas as pl
from jax.experimental.pallas import tpu as pltpu
from jax.sharding import PartitionSpec as P

HALO = 128
ROWS = 8
F32 = jnp.float32
BF16 = jnp.bfloat16


def make_tables(width):
    index = np.arange(width)
    angle = (index[:, None] * index[None, :] % width) * (2.0 * math.pi / width)
    both = np.concatenate([np.cos(angle), np.sin(angle)], axis=0) / math.sqrt(width)
    high = both.astype(ml_dtypes.bfloat16)
    low = (both - high.astype(np.float64)).astype(ml_dtypes.bfloat16)
    right = np.concatenate([high, high, low], axis=0)
    return jnp.asarray(right), jnp.asarray(np.ascontiguousarray(right.T))


def split_field(field):
    high = field.astype(BF16)
    low = (field - high.astype(F32)).astype(BF16)
    return high, low


def transform(real_part, imag_part, right, left, forward):
    width = real_part.shape[0]

    def arrange(r, i, axis):
        if forward:
            top = jnp.concatenate([r, i], axis=axis)
            bottom = jnp.concatenate([i, -r], axis=axis)
        else:
            top = jnp.concatenate([r, -i], axis=axis)
            bottom = jnp.concatenate([i, r], axis=axis)
        return jnp.concatenate([top, bottom], axis=1 - axis)

    rh, rl = split_field(real_part)
    ih, il = split_field(imag_part)
    high = arrange(rh, ih, 1)
    field = jnp.concatenate([high, arrange(rl, il, 1), high], axis=1)
    mid = jnp.dot(field, right[...], preferred_element_type=F32)
    rh, rl = split_field(mid[:width])
    ih, il = split_field(mid[width:])
    high = arrange(rh, ih, 0)
    field = jnp.concatenate([high, arrange(rl, il, 0), high], axis=0)
    out = jnp.dot(left[...], field, preferred_element_type=F32)
    return out[:, :width], out[:, width:]


def complex_product(a_real, a_imag, b_real, b_imag):
    return (a_real * b_real - a_imag * b_imag, a_real * b_imag + a_imag * b_real)


def conj_product(a_real, a_imag, b_real, b_imag):
    return (a_real * b_real + a_imag * b_imag, a_real * b_imag - a_imag * b_real)


def local_kernel(
    layers, shifts, mid, west, east, north, south, ncorn, scorn, illum, filt, seen, right, left,
    g_mid, g_west, g_east, g_north, g_south, g_ncorn, g_scorn, g_probe,
    ext, acc, win,
):
    tile = mid.shape[1]
    width = illum.shape[1]
    places = seen.shape[0]
    a, b = HALO, HALO + tile
    e = b + HALO
    parts = (
        (mid, slice(a, b), slice(a, b), None),
        (west, slice(a, b), slice(0, a), None),
        (east, slice(a, b), slice(b, e), None),
        (north, slice(0, a), slice(a, b), None),
        (south, slice(b, e), slice(a, b), None),
        (ncorn, slice(0, a), slice(0, a), 0),
        (ncorn, slice(0, a), slice(b, e), 1),
        (scorn, slice(b, e), slice(0, a), 0),
        (scorn, slice(b, e), slice(b, e), 1),
    )
    for ref, rows, cols, side in parts:
        ext[:, rows, cols] = ref[...] if side is None else ref[side]
    acc[...] = jnp.zeros_like(acc)
    g_probe[...] = jnp.zeros_like(g_probe)

    @pl.loop(0, places)
    def _(p):
        start_row = shifts[p, 0] + HALO
        start_col = shifts[p, 1] + HALO
        block = jnp.where(start_col > HALO, 1, 0)
        base = pl.multiple_of(block * HALO, HALO)
        rest = start_col - base
        span = width + HALO
        first = pl.multiple_of(start_row // ROWS * ROWS, ROWS)
        over = start_row - first
        tall = width + ROWS
        rows = pl.ds(first, tall)
        for c in range(2 * layers):
            wide = ext[c, rows, pl.ds(base, span)]
            wide = pltpu.roll(wide, lax.rem(tall - over, tall), 0)[:width]
            win[c] = pltpu.roll(wide, lax.rem(span - rest, span), 1)[:, :width]
        wave = (illum[0], illum[1])
        saved = []
        for layer in range(layers):
            saved.append(wave)
            out = complex_product(*wave, win[2 * layer], win[2 * layer + 1])
            if layer + 1 < layers:
                spec = transform(*out, right, left, True)
                spec = complex_product(*spec, filt[0], filt[1])
                wave = transform(*spec, right, left, False)
        far_real, far_imag = transform(*out, right, left, True)
        misfit = far_real * far_real + far_imag * far_imag - seen[p]
        back = transform(misfit * far_real, misfit * far_imag, right, left, False)
        for layer in reversed(range(layers)):
            grads = conj_product(*saved[layer], *back)
            for k in range(2):
                wide = jnp.concatenate([grads[k], jnp.zeros((width, HALO), F32)], axis=1)
                wide = pltpu.roll(wide, rest, 1)
                wide = jnp.concatenate([wide, jnp.zeros((ROWS, span), F32)], axis=0)
                wide = pltpu.roll(wide, over, 0)
                acc[2 * layer + k, rows, pl.ds(base, span)] += wide
            head = conj_product(win[2 * layer], win[2 * layer + 1], *back)
            if layer > 0:
                spec = transform(*head, right, left, True)
                spec = conj_product(filt[0], filt[1], *spec)
                back = transform(*spec, right, left, False)
        g_probe[0] += head[0]
        g_probe[1] += head[1]

    outs = (g_mid, g_west, g_east, g_north, g_south, g_ncorn, g_ncorn, g_scorn, g_scorn)
    for (_, rows, cols, side), out in zip(parts, outs):
        if side is None:
            out[...] = acc[:, rows, cols]
        else:
            out[side] = acc[:, rows, cols]


def local_gradients(layers, shifts, pieces, illum, filt, seen, right, left):
    chans, tile = pieces[0].shape[:2]
    width = illum.shape[1]
    side = tile + 2 * HALO
    vmem = pl.BlockSpec(memory_space=pltpu.VMEM)
    shapes = [x.shape for x in pieces] + [illum.shape]
    return pl.pallas_call(
        functools.partial(local_kernel, layers),
        out_shape=[jax.ShapeDtypeStruct(s, F32) for s in shapes],
        in_specs=[pl.BlockSpec(memory_space=pltpu.SMEM)] + [vmem] * 12,
        out_specs=[vmem] * 8,
        scratch_shapes=[
            pltpu.VMEM((chans, side + ROWS, side), F32),
            pltpu.VMEM((chans, side + ROWS, side), F32),
            pltpu.VMEM((chans, width, width), F32),
        ],
        compiler_params=pltpu.CompilerParams(vmem_limit_bytes=34 * 2**20),
        name="local_gradients",
    )(shifts, *pieces, illum, filt, seen, right, left)


def remote(src, dst, sems, slot, device):
    return pltpu.make_async_remote_copy(
        src_ref=src,
        dst_ref=dst,
        send_sem=sems.at[0, slot],
        recv_sem=sems.at[1, slot],
        device_id=device,
        device_id_type=pl.DeviceIdType.MESH,
    )


def greet(peers):
    barrier = pltpu.get_barrier_semaphore()
    for device in peers:
        pl.semaphore_signal(barrier, inc=1, device_id=device, device_id_type=pl.DeviceIdType.MESH)
    pl.semaphore_wait(barrier, len(peers))


def halo_kernel(
    chans, count, across, mid, angle, west, east, north, south, ncorn, scorn, filt, sems
):
    tile_rows, tile_cols = mid.shape[1:]
    row, col = lax.axis_index("row"), lax.axis_index("col")
    below = (lax.rem(row + 1, count), col)
    above = (lax.rem(row + count - 1, count), col)
    toeast = (row, lax.rem(col + 1, across))
    towest = (row, lax.rem(col + across - 1, across))
    greet([below, above, toeast, towest])
    last_rows = pl.ds(tile_rows - HALO, HALO)
    first_rows = pl.ds(0, HALO)
    last_cols = pl.ds(tile_cols - HALO, HALO)
    first_cols = pl.ds(0, HALO)
    sides, rows, corners = [], [], []
    for l in range(chans):
        ch = pl.ds(l, 1)
        slot = 8 * l
        sides.append((
            remote(mid.at[ch, :, last_cols], west.at[ch], sems, slot, toeast),
            remote(mid.at[ch, :, first_cols], east.at[ch], sems, slot + 1, towest),
        ))
        rows.append(remote(mid.at[ch, last_rows], north.at[ch], sems, slot + 2, below))
        rows.append(remote(mid.at[ch, first_rows], south.at[ch], sems, slot + 3, above))
        for k, ref in enumerate((west, east)):
            corners.append((
                remote(ref.at[ch, last_rows], ncorn.at[k, ch], sems, slot + 4 + k, below),
                remote(ref.at[ch, first_rows], scorn.at[k, ch], sems, slot + 6 + k, above),
            ))
    for pair in sides:
        for copy in pair:
            copy.start()
    for copy in rows:
        copy.start()
    filt[0] = jnp.cos(angle[...])
    filt[1] = jnp.sin(angle[...])
    for l in range(chans):
        for k in range(2):
            sides[l][k].wait_recv()
            for copy in corners[2 * l + k]:
                copy.start()
    for copy in rows:
        copy.wait()
    for pair in corners:
        for copy in pair:
            copy.wait()
    for pair in sides:
        for copy in pair:
            copy.wait_send()


def fetch_halo(mid, angle):
    count, across = lax.axis_size("row"), lax.axis_size("col")
    chans, tile_rows, tile_cols = mid.shape
    side = (chans, tile_rows, HALO)
    flat = (chans, HALO, tile_cols)
    corner = (2, chans, HALO, HALO)
    vmem = pl.BlockSpec(memory_space=pltpu.VMEM)
    return pl.pallas_call(
        functools.partial(halo_kernel, chans, count, across),
        out_shape=[
            jax.ShapeDtypeStruct(s, F32)
            for s in (side, side, flat, flat, corner, corner, (2, *angle.shape))
        ],
        in_specs=[vmem] * 2,
        out_specs=[vmem] * 7,
        scratch_shapes=[pltpu.SemaphoreType.DMA((2, 8 * chans))],
        compiler_params=pltpu.CompilerParams(
            collective_id=0, has_side_effects=True, vmem_limit_bytes=24 * 2**20
        ),
        name="fetch_halo",
    )(mid, angle)


def settle_kernel(
    chans, count, across,
    g_mid, g_west, g_east, g_north, g_south, g_ncorn, g_scorn, g_probe, out, probe,
    south_corn, north_corn, side_send, side_recv, south_mid, north_mid,
    probe_rows, probe_send, probe_cols, sems, row_sems, col_sems,
):
    tile_rows, tile_cols = out.shape[1:]
    row, col = lax.axis_index("row"), lax.axis_index("col")
    row_peers = [(lax.rem(row + d, count), col) for d in range(1, count)]
    col_peers = [(row, lax.rem(col + d, across)) for d in range(1, across)]
    below, above = row_peers[0], row_peers[-1]
    toeast, towest = col_peers[0], col_peers[-1]
    greet(row_peers + col_peers)
    last_rows = pl.ds(tile_rows - HALO, HALO)
    first_rows = pl.ds(0, HALO)
    corners, mids = [], []
    for l in range(chans):
        ch = pl.ds(l, 1)
        slot = 8 * l
        for k in range(2):
            corners.append((l, k, (
                remote(g_ncorn.at[k, ch], south_corn.at[k, ch], sems, slot + k, above),
                remote(g_scorn.at[k, ch], north_corn.at[k, ch], sems, slot + 2 + k, below),
            )))
        mids.append((l, (
            remote(g_north.at[ch], south_mid.at[ch], sems, slot + 4, above),
            remote(g_south.at[ch], north_mid.at[ch], sems, slot + 5, below),
        )))
    for _, _, pair in corners:
        for copy in pair:
            copy.start()
    sides = []
    for l, k, pair in corners:
        ch = pl.ds(l, 1)
        for copy in pair:
            copy.wait_recv()
        side_send[k, ch] = (g_west, g_east)[k][ch]
        side_send[k, ch, last_rows] += south_corn[k, ch]
        side_send[k, ch, first_rows] += north_corn[k, ch]
        copy = remote(
            side_send.at[k, ch], side_recv.at[k, ch], sems, 8 * l + 6 + k, (towest, toeast)[k]
        )
        copy.start()
        sides.append((l, k, copy))
    strip = probe.shape[1]
    row_copies = []
    for d in range(1, count):
        device = row_peers[d - 1]
        part = pl.ds(pl.multiple_of(device[0] * strip, strip), strip)
        copy = remote(g_probe.at[:, part], probe_rows.at[d - 1], row_sems, d - 1, device)
        copy.start()
        row_copies.append(copy)
    for _, pair in mids:
        for copy in pair:
            copy.start()
    total = g_probe[:, pl.ds(pl.multiple_of(row * strip, strip), strip)]
    for d, copy in enumerate(row_copies):
        copy.wait_recv()
        total += probe_rows[d]
    narrow = probe.shape[2]
    for c in range(across):
        probe_send[c] = total[:, :, c * narrow : (c + 1) * narrow]
    col_copies = []
    for d in range(1, across):
        device = col_peers[d - 1]
        copy = remote(probe_send.at[device[1]], probe_cols.at[d - 1], col_sems, d - 1, device)
        copy.start()
        col_copies.append(copy)
    out[...] = g_mid[...]
    for l, pair in mids:
        ch = pl.ds(l, 1)
        for copy in pair:
            copy.wait_recv()
        out[ch, last_rows] += south_mid[ch]
        out[ch, first_rows] += north_mid[ch]
    for l, k, copy in sides:
        ch = pl.ds(l, 1)
        cols = pl.ds((tile_cols - HALO) * (1 - k), HALO)
        copy.wait_recv()
        out[ch, :, cols] += side_recv[k, ch]
    part = probe_send[col]
    for d, copy in enumerate(col_copies):
        copy.wait_recv()
        part += probe_cols[d]
    probe[...] = part
    for _, _, pair in corners:
        for copy in pair:
            copy.wait_send()
    for _, pair in mids:
        for copy in pair:
            copy.wait_send()
    for _, _, copy in sides:
        copy.wait_send()
    for copy in row_copies + col_copies:
        copy.wait_send()


def settle(grads):
    count, across = lax.axis_size("row"), lax.axis_size("col")
    chans, tile_rows, tile_cols = grads[0].shape
    width = grads[7].shape[1]
    strip, narrow = width // count, width // across
    vmem = pl.BlockSpec(memory_space=pltpu.VMEM)
    dma = pltpu.SemaphoreType.DMA
    return pl.pallas_call(
        functools.partial(settle_kernel, chans, count, across),
        out_shape=[
            jax.ShapeDtypeStruct((chans, tile_rows, tile_cols), F32),
            jax.ShapeDtypeStruct((2, strip, narrow), F32),
        ],
        in_specs=[vmem] * 8,
        out_specs=[vmem] * 2,
        scratch_shapes=[
            pltpu.VMEM((2, chans, HALO, HALO), F32),
            pltpu.VMEM((2, chans, HALO, HALO), F32),
            pltpu.VMEM((2, chans, tile_rows, HALO), F32),
            pltpu.VMEM((2, chans, tile_rows, HALO), F32),
            pltpu.VMEM((chans, HALO, tile_cols), F32),
            pltpu.VMEM((chans, HALO, tile_cols), F32),
            pltpu.VMEM((count - 1, 2, strip, width), F32),
            pltpu.VMEM((across, 2, strip, narrow), F32),
            pltpu.VMEM((across - 1, 2, strip, narrow), F32),
            dma((2, 8 * chans)),
            dma((2, count - 1)),
            dma((2, across - 1)),
        ],
        compiler_params=pltpu.CompilerParams(
            collective_id=1, has_side_effects=True, vmem_limit_bytes=30 * 2**20
        ),
        name="settle_gradients",
    )(*grads)


def body(specimen_transmit, illumination, fresnel_angle, recorded_intensity, frame_shifts):
    layers = specimen_transmit.shape[0]
    tile = specimen_transmit.shape[2]
    width = illumination.shape[1]
    right, left = make_tables(width)
    mid = specimen_transmit.reshape(2 * layers, tile, specimen_transmit.shape[3])
    *halo, filt = fetch_halo(mid, fresnel_angle)
    pieces = (mid, *halo)
    grads = local_gradients(
        layers, frame_shifts[0, 0], pieces, illumination, filt, recorded_intensity[0, 0], right, left
    )
    result, probe_part = settle(grads)
    return (result.reshape(specimen_transmit.shape), probe_part)


def solution(mesh):
    placed = (
        P(None, None, "row", "col"),
        P(),
        P(),
        P("row", "col", None, None, None),
        P("row", "col", None, None),
    )
    return jax.shard_map(
        body,
        mesh=mesh,
        in_specs=placed,
        out_specs=(P(None, None, "row", "col"), P(None, "row", "col")),
        check_vma=False,
    )
```
